512 devices in a mesh: seq: 32 (over x, y), tensor: 4 (over z_lo, core), dp: 4 (over z_hi).
Axes of the slice: x: 4, y: 8, z: 8 (z_hi: 4, z_lo: 2; z = z_hi * 2 + z_lo), core: 2. Of those that a mesh axis runs over, the one named last changes fastest.
Arguments:
- frames_in: bfloat16 [4, 32, 256, 3072], P('dp', 'seq', None, 'tensor'), parts along dimension 0, may hold values from -6 to 6
- norm_gain: float32 [3072], replicated, may hold values from 0.5 to 6
- w_qkv: bfloat16 [3072, 3, 2048], P('seq', None, 'tensor'), may hold values from -0.109375 to 0.109375
- w_out: bfloat16 [2048, 3072], P('tensor'), may hold values from -0.125 to 0.125
Outputs:
- mixed: bfloat16 [4, 32, 256, 3072], P('dp', 'seq', None, 'tensor'), parts along dimension 0
The draws below stay inside these ranges and needn't reach their ends.
There are 4 independent parts, one for each index of `dp`. The reference program is written for one: setup_inputs(seed, part) draws one part's arguments, and reference() takes and returns one part's arrays. A program takes and returns all parts, laid end to end along the dimension named above; an argument that names none is the same for every part. Nothing has to cross between parts.
All inputs are finite; a program needn't handle non-finite values.
Results may differ from the reference program's by a relative error of at most 0.019.
Values may be sent and summed in bfloat16 or wider, within the bound.
No kernel may reach another device: no remote copies, remote signals or barrier semaphores. Data moves between devices by JAX's collectives and lax.ppermute only.
A program may use at most 64 MiB of HBM per device.

```python
import jax
import jax.numpy as jnp
from jax import lax

D = 3072
H = 16
HD = 128
CLIPS = 1
FRAMES = 32
PATCHES = 256
N_TENSOR = 4


def draw_norm_gain(key, part):
    key = jax.random.fold_in(key, 7)
    values = jax.random.uniform(key, (D,), jnp.float32, 0.5, 1.5)
    return values


def levels(key, dims, shards, low, top_value):
    loudness = 1.0
    for dim, shards_of in shards:
        steps = jax.random.uniform(jax.random.fold_in(jax.random.fold_in(key, 6), dim), (shards_of,), jnp.float32, low / len(shards), top_value / len(shards))
        loudness = loudness * jnp.repeat(jnp.exp(steps), dims[dim] // shards_of).reshape((-1,) + (1,) * (len(dims) - 1 - dim))
    return loudness


def bell_draw(stream_key, extent, deviation, limit, shards=(), dtype=jnp.bfloat16):
    array = jax.random.normal(stream_key, extent, jnp.float32) * deviation
    if len(shards) > 0:
        array = levels(stream_key, extent, shards, -0.22, 0.18) * array
    return jnp.clip(array, min=-limit, max=limit).astype(dtype)


def setup_inputs(seed: int = 0, part: int = 0) -> dict:
    seeds = jax.random.split(jax.random.key(seed), 5)
    part_keys = jax.random.split(jax.random.fold_in(seeds[4], part), 5)
    return {
        "frames_in": bell_draw(part_keys[0], (CLIPS, FRAMES, PATCHES, D), 1.0, 6.0, ((1, 32), (3, 4))),
        "norm_gain": draw_norm_gain(jax.random.fold_in(seeds[4], 71), part),
        "w_qkv": bell_draw(seeds[2], (D, 3, H * HD), D ** -0.5, 0.109375, ((0, 32), (2, 4))),
        "w_out": bell_draw(seeds[3], (H * HD, D), (H * HD) ** -0.5, 0.125, ((0, 4),)),
    }


def reference(frames_in, norm_gain, w_qkv, w_out):
    widened = frames_in.astype(jnp.float32)
    average = lax.optimization_barrier(jnp.mean(widened, axis=-1, keepdims=True))
    centred = widened - average
    spread = lax.optimization_barrier(jnp.mean(centred * centred, axis=-1, keepdims=True))
    normed = (centred * lax.rsqrt(spread + 1e-06) * norm_gain).astype(jnp.bfloat16)
    token_rows = normed.reshape(-1, D)
    projected = jnp.dot(token_rows, w_qkv.reshape(D, 3 * H * HD), preferred_element_type=jnp.float32)
    projected = projected.astype(jnp.bfloat16).reshape(CLIPS, FRAMES, PATCHES, 3, H, HD)
    queries = projected[:, :, :, 0].astype(jnp.float32)
    key_part = projected[:, :, :, 1].astype(jnp.float32)
    value_part = projected[:, :, :, 2].astype(jnp.float32)
    scores = jnp.einsum('cfphd,cgphd->cphfg', queries, key_part) * HD ** (-0.5)
    weights = jax.nn.softmax(scores, axis=-1).astype(jnp.bfloat16)
    attended = jnp.einsum('cphfg,cgphd->cfphd', weights.astype(jnp.float32), value_part)
    attended = attended.astype(jnp.bfloat16).reshape(-1, H * HD)
    group_width = H // N_TENSOR * HD
    summed = jnp.zeros((attended.shape[0], D), jnp.float32)
    for group in range(N_TENSOR):
        lower = group * group_width
        partial_value = jnp.dot(attended[:, lower:lower + group_width], w_out[lower:lower + group_width], preferred_element_type=jnp.float32)
        summed = summed + partial_value.astype(jnp.bfloat16).astype(jnp.float32)
    return (widened + summed.reshape(widened.shape)).astype(jnp.bfloat16)
```

```python
import jax
import jax.numpy as jnp
from jax import lax
from jax.experimental import pallas as pl
from jax.experimental.pallas import tpu as pltpu
from jax.sharding import Mesh, PartitionSpec as P

HD = 128
WIDTH = 3072
QUARTER = 768
F32 = jnp.float32
BF16 = jnp.bfloat16
VMEM = pl.BlockSpec(memory_space=pltpu.VMEM)
SMEM = pl.BlockSpec(memory_space=pltpu.SMEM)


def ring(size, shift):
    return [(i, (i + shift) % size) for i in range(size)]


def swap(value, axis):
    return lax.ppermute(value, axis, [(0, 1), (1, 0)])


def normalize_block(x, z, near, far, gain, store):
    parts = []
    for z_far, side in enumerate((near, far)):
        for core in range(2):
            piece = side[:, 16 * core : 16 * core + 16, :].reshape(128, QUARTER).astype(F32)
            parts.append((2 * lax.rem(z + z_far, 2) + core, piece))
    total = parts[0][1] + parts[1][1] + parts[2][1] + parts[3][1]
    average = jnp.sum(total, axis=-1, keepdims=True) * (1.0 / WIDTH)
    squares = 0.0
    for _, value in parts:
        centred = value - average
        squares = squares + centred * centred
    spread = jnp.sum(squares, axis=-1, keepdims=True) * (1.0 / WIDTH)
    scale = lax.rsqrt(spread + 1e-06)
    for q, value in parts:
        store(q, ((value - average) * scale * gain[q]).astype(BF16))


def normalize_kernel(place, xa, xb, la, lb, ra, rb, gain, out):
    for block, (near, far) in enumerate(((xa, xb), (la, lb), (ra, rb))):

        def store(q, value, block=block):
            out[q, block] = value

        normalize_block(place[0], place[1], near, far, gain, store)


def attend_kernel(place, normed, oa, ob, gain, w_rows, out, last):
    x, z, c = place[0], place[1], place[2]

    def store(q, value):
        last[q] = value

    normalize_block(x, z, oa, ob, gain, store)
    sides = [jnp.zeros((512, 3 * HD), F32) for _ in range(2)]
    for k in range(4):
        q = lax.rem(x + 4 - k, 4)
        tokens = jnp.concatenate([normed[q].reshape(384, QUARTER), last[q]], axis=0)
        for core in range(2):
            weight = w_rows[k, QUARTER * core : QUARTER * core + QUARTER]
            sides[core] = sides[core] + jnp.dot(tokens, weight, preferred_element_type=F32)

    row = lax.broadcasted_iota(jnp.int32, (512, 512), 0)
    column = lax.broadcasted_iota(jnp.int32, (512, 512), 1)
    same_patch = lax.rem(row, 16) == lax.rem(column, 16)
    heads = []
    for projected in sides:
        query = projected[:, :HD].astype(BF16)
        key = projected[:, HD : 2 * HD].astype(BF16)
        value = projected[:, 2 * HD :].astype(BF16)
        scores = lax.dot_general(query, key, (((1,), (1,)), ((), ())), preferred_element_type=F32)
        scores = jnp.where(same_patch, scores * HD**-0.5, -jnp.inf)
        top = jnp.max(scores, axis=-1, keepdims=True)
        weights = jnp.exp(scores - top)
        weights = (weights / jnp.sum(weights, axis=-1, keepdims=True)).astype(BF16)
        heads.append(jnp.dot(weights, value, preferred_element_type=F32).astype(BF16))
    both = jnp.concatenate(heads, axis=1)
    for block, shift in enumerate((0, 3, 1, 2)):
        piece = both[128 * block : 128 * block + 128].reshape(8, 16, 2 * HD)
        frame = lax.rem(x + shift, 4)
        out[frame, :, 0] = piece
        out[frame, :, 1] = piece


def output_kernel(place, near, far, wo00, wo10, wo01, wo11, residual, out):
    z, c = place[1], place[2]
    total = jnp.zeros((256, QUARTER), F32)
    for z_far, weights in enumerate(((wo00, wo01), (wo10, wo11))):
        source = lax.rem(z + z_far, 2)
        for core in range(2):
            pieces = []
            for half in (near, far):
                columns = [
                    half[s, :, source, :, HD * core : HD * core + HD].reshape(128, HD) for s in range(4)
                ]
                pieces.append(jnp.concatenate(columns, axis=1))
            attended = jnp.concatenate(pieces, axis=0)
            weight = jnp.where(c == core, weights[0][...], weights[1][...])
            total = total + jnp.dot(attended, weight, preferred_element_type=F32)
    for half in range(2):
        side = lax.rem(c + half, 2)
        mixed = residual[:, side].astype(F32) + total[128 * half : 128 * half + 128].reshape(8, 16, QUARTER)
        out[:, side] = mixed.astype(BF16)


def slice_kernel(place, source, *outs):
    for k, out in enumerate(outs):
        head = lax.rem(place[0] + k, 4)
        for part in range(3):
            out[:, HD * part : HD * part + HD] = source[part, :, pl.ds(pl.multiple_of(head * HD, HD), HD)]


def after(value, *others):
    return lax.optimization_barrier((value, *others))[0]


def kernel_call(kernel, shapes, operands, flops, moved, scratch=()):
    return pl.pallas_call(
        kernel,
        out_shape=shapes,
        in_specs=[SMEM] + [VMEM] * (len(operands) - 1),
        out_specs=jax.tree.map(lambda _: VMEM, shapes),
        scratch_shapes=list(scratch),
        compiler_params=pltpu.CompilerParams(vmem_limit_bytes=40 * 2**20),
        cost_estimate=pl.CostEstimate(flops=flops, bytes_accessed=moved, transcendentals=0),
    )(*operands)


def body(frames_in, norm_gain, w_qkv, w_out):
    x, z, c = lax.axis_index("x"), lax.axis_index("z"), lax.axis_index("c")
    place = jnp.stack([x, z, c]).astype(jnp.int32)
    gain = norm_gain.reshape(4, 1, QUARTER)

    slots = kernel_call(
        slice_kernel,
        [jax.ShapeDtypeStruct((96, 3 * HD), BF16)] * 4,
        (place, w_qkv.transpose(1, 0, 2)),
        0,
        6 * 10**5,
    )
    w_rows = [slots[0]] + [lax.ppermute(slots[k], "x", ring(4, k)) for k in (1, 2, 3)]
    w_rows = lax.all_gather(jnp.stack(w_rows), ("c", "y"), axis=1, tiled=True)

    tokens = frames_in.reshape(16, 16, QUARTER)
    xa = lax.all_to_all(tokens, ("y", "c"), 0, 0, tiled=True).reshape(8, 32, QUARTER)
    xb = swap(xa, "z")
    la, ra, oa = (lax.ppermute(xa, "x", ring(4, shift)) for shift in (1, 3, 2))
    lb, rb, ob = (lax.ppermute(xb, "x", ring(4, shift)) for shift in (1, 3, 2))

    normed = kernel_call(
        normalize_kernel,
        jax.ShapeDtypeStruct((4, 3, 128, QUARTER), BF16),
        (place, xa, xb, la, lb, ra, rb, gain),
        10**7,
        5 * 10**6,
    )
    attended = kernel_call(
        attend_kernel,
        jax.ShapeDtypeStruct((4, 8, 2, 16, 2 * HD), BF16),
        (place, normed, oa, ob, gain, w_rows),
        3 * 10**9,
        9 * 10**6,
        [pltpu.VMEM((4, 128, QUARTER), BF16)],
    )

    def half(value, index, size):
        return lax.dynamic_slice_in_dim(value, index * size, size, axis=1)

    wo_keep = half(w_out, z, 2 * QUARTER)
    wo_got = swap(after(half(w_out, 1 - z, 2 * QUARTER), xb), "z")
    wo00, wo10 = half(wo_keep, c, QUARTER), half(wo_got, c, QUARTER)
    wo01, wo11 = swap(half(wo_keep, 1 - c, QUARTER), "c"), swap(half(wo_got, 1 - c, QUARTER), "c")

    attended = lax.all_to_all(attended.reshape(64, 16, 2 * HD), ("x", "y", "z"), 0, 0, tiled=True)
    other = swap(attended, "c")
    shape = (4, 8, 2, 16, 2 * HD)
    mixed = kernel_call(
        output_kernel,
        jax.ShapeDtypeStruct((8, 2, 16, QUARTER), BF16),
        (
            place,
            attended.reshape(shape),
            other.reshape(shape),
            wo00,
            wo10,
            wo01,
            wo11,
            frames_in.reshape(8, 2, 16, QUARTER),
        ),
        8 * 10**8,
        6 * 10**6,
    )
    return mixed.reshape(1, 1, 256, QUARTER)


def solution(mesh):
    fine = Mesh(mesh.devices.reshape(4, 8, 2, 2, 4), ("x", "y", "z", "c", "dp"))
    seq, tensor = ("x", "y"), ("z", "c")
    in_specs = (P("dp", seq, None, tensor), P(), P(seq, None, tensor), P(tensor, None))
    out_specs = P("dp", seq, None, tensor)
    return jax.shard_map(body, mesh=fine, in_specs=in_specs, out_specs=out_specs, check_vma=False)
```

```python
import jax
import jax.numpy as jnp
from jax import lax
from jax.experimental import pallas as pl
from jax.experimental.pallas import tpu as pltpu
from jax.sharding import Mesh, PartitionSpec as P

HD = 128
WIDTH = 3072
QUARTER = 768
F32 = jnp.float32
BF16 = jnp.bfloat16
VMEM = pl.BlockSpec(memory_space=pltpu.VMEM)
ANY = pl.BlockSpec(memory_space=pl.ANY)
SMEM = pl.BlockSpec(memory_space=pltpu.SMEM)


def ring(size, shift):
    return [(i, (i + shift) % size) for i in range(size)]


def swap(value, axis):
    return lax.ppermute(value, axis, [(0, 1), (1, 0)])


def normalize_block(z, near, far, gain, store):
    parts = []
    for z_far, side in enumerate((near, far)):
        for core in range(2):
            quarter = 2 * lax.rem(z + z_far, 2) + core
            piece = side[:, 16 * core : 16 * core + 16, :].reshape(128, QUARTER).astype(F32)
            parts.append((quarter, piece))
    total = parts[0][1] + parts[1][1] + parts[2][1] + parts[3][1]
    average = jnp.sum(total, axis=-1, keepdims=True) * (1.0 / WIDTH)
    squares = 0.0
    for _, value in parts:
        centred = value - average
        squares = squares + centred * centred
    spread = jnp.sum(squares, axis=-1, keepdims=True) * (1.0 / WIDTH)
    scale = lax.rsqrt(spread + 1e-06)
    for q, value in parts:
        store(q, ((value - average) * scale * gain[q]).astype(BF16))


def attend(projected):
    row = lax.broadcasted_iota(jnp.int32, (256, 256), 0)
    column = lax.broadcasted_iota(jnp.int32, (256, 256), 1)
    same_patch = lax.rem(row, 8) == lax.rem(column, 8)
    heads = []
    for core in range(2):
        groups = []
        for group in range(2):

            def pick(part, core=core, group=group):
                first = (3 * core + part) * HD
                rows = projected[:, first : first + HD].reshape(32, 16, HD)
                return rows[:, 8 * group : 8 * group + 8].reshape(256, HD).astype(BF16)

            query, key, value = pick(0), pick(1), pick(2)
            scores = lax.dot_general(query, key, (((1,), (1,)), ((), ())), preferred_element_type=F32)
            scores = jnp.where(same_patch, scores * HD**-0.5, -jnp.inf)
            weights = jnp.exp(scores - jnp.max(scores, axis=-1, keepdims=True))
            weights = (weights / jnp.sum(weights, axis=-1, keepdims=True)).astype(BF16)
            groups.append(jnp.dot(weights, value, preferred_element_type=F32).reshape(32, 8, HD))
        heads.append(jnp.concatenate(groups, axis=1))
    return jnp.concatenate(heads, axis=2).astype(BF16)


def attend_kernel(place, xa, xb, la, lb, ra, rb, oa_hbm, ob_hbm, gain, w_hbm, out, *scratch):
    opposite, normed, w_rows, projected, opposite_sent, w_sent = scratch
    x, z = place[0], place[1]
    copies = [
        pltpu.make_async_copy(source, opposite.at[i], opposite_sent.at[i])
        for i, source in enumerate((oa_hbm, ob_hbm))
    ]
    for k in range(4):
        for core in range(2):
            target = w_rows.at[pl.ds(QUARTER * k, QUARTER), pl.ds(3 * HD * core, 3 * HD)]
            source = w_hbm.at[k, pl.ds(QUARTER * core, QUARTER)]
            copies.append(pltpu.make_async_copy(source, target, w_sent.at[2 * k + core]))
    for copy in copies:
        copy.start()
    blocks = ((xa, xb), (la, lb), (ra, rb), (opposite.at[0], opposite.at[1]))
    for i, (near, far) in enumerate(blocks):
        rows = slice(128 * i, 128 * i + 128)

        def store(q, value, rows=rows):
            slot = pl.multiple_of(lax.rem(x + 4 - q, 4) * QUARTER, QUARTER)
            normed[rows, pl.ds(slot, QUARTER)] = value

        normalize_block(z, near, far, gain, store)
        if i == 1:
            for copy in copies:
                copy.wait()
            projected[:128] = jnp.dot(normed[:128], w_rows[...], preferred_element_type=F32)
        if i >= 1:
            projected[rows] = jnp.dot(normed[rows], w_rows[...], preferred_element_type=F32)
    attended = attend(projected[...])
    for i, shift in enumerate((0, 3, 1, 2)):
        frame = lax.rem(x + shift, 4)
        for chip in range(2):
            out[frame, :, chip] = attended[8 * i : 8 * i + 8]


def output_kernel(place, near, far, wo00, wo10, wo01, wo11, residual, out):
    z, c = place[1], place[2]
    total = jnp.zeros((256, QUARTER), F32)
    for z_far, weights in enumerate(((wo00, wo01), (wo10, wo11))):
        source = lax.rem(z + z_far, 2)
        for core in range(2):
            pieces = []
            for half in (near, far):
                columns = [
                    half[s, :, source, :, HD * core : HD * core + HD].reshape(128, HD) for s in range(4)
                ]
                pieces.append(jnp.concatenate(columns, axis=1))
            attended = jnp.concatenate(pieces, axis=0)
            weight = jnp.where(c == core, weights[0][...], weights[1][...])
            total = total + jnp.dot(attended, weight, preferred_element_type=F32)
    for half in range(2):
        side = lax.rem(c + half, 2)
        mixed = residual[:, side].astype(F32) + total[128 * half : 128 * half + 128].reshape(8, 16, QUARTER)
        out[:, side] = mixed.astype(BF16)


def slice_kernel(place, source, *outs):
    for k, out in enumerate(outs):
        head = lax.rem(place[0] + k, 4)
        for part in range(3):
            out[:, HD * part : HD * part + HD] = source[part, :, pl.ds(pl.multiple_of(head * HD, HD), HD)]


def after(value, *others):
    return lax.optimization_barrier((value, *others))[0]


def kernel_call(kernel, shapes, operands, flops, moved, mebibytes, scratch=(), left_out=()):
    return pl.pallas_call(
        kernel,
        out_shape=shapes,
        in_specs=[
            SMEM if value.dtype == jnp.int32 else ANY if i in left_out else VMEM
            for i, value in enumerate(operands)
        ],
        out_specs=jax.tree.map(lambda _: VMEM, shapes),
        scratch_shapes=list(scratch),
        compiler_params=pltpu.CompilerParams(vmem_limit_bytes=mebibytes * 2**20),
        cost_estimate=pl.CostEstimate(flops=flops, bytes_accessed=moved, transcendentals=0),
    )(*operands)


def body(frames_in, norm_gain, w_qkv, w_out):
    x, z, c = lax.axis_index("x"), lax.axis_index("z"), lax.axis_index("c")
    place = jnp.stack([x, z, c]).astype(jnp.int32)
    gain = norm_gain.reshape(4, 1, QUARTER)

    slots = kernel_call(
        slice_kernel,
        [jax.ShapeDtypeStruct((96, 3 * HD), BF16)] * 4,
        (place, w_qkv.transpose(1, 0, 2)),
        0,
        6 * 10**5,
        4,
    )
    w_rows = [slots[0]] + [lax.ppermute(slots[k], "x", ring(4, k)) for k in (1, 2, 3)]
    w_rows = jnp.stack(w_rows)

    tokens = frames_in.reshape(16, 16, QUARTER)
    xa = lax.all_to_all(tokens, ("y", "c"), 0, 0, tiled=True).reshape(8, 32, QUARTER)
    xa, w_rows = lax.optimization_barrier((xa, w_rows))
    w_rows = lax.all_gather(w_rows, ("c", "y"), axis=1, tiled=True)
    xb = swap(xa, "z")
    la, ra, oa = (lax.ppermute(xa, "x", ring(4, shift)) for shift in (1, 3, 2))
    xb_late = after(xb, la, ra)
    lb, rb, ob = (lax.ppermute(xb_late, "x", ring(4, shift)) for shift in (1, 3, 2))

    def half(value, index, size):
        return lax.dynamic_slice_in_dim(value, index * size, size, axis=1)

    columns = [2 * z + c, 2 * z + 1 - c]
    far_columns = [2 * (1 - z) + c, 2 * (1 - z) + 1 - c]
    w_late = after(w_out, xb)
    wo00 = half(w_out, columns[0], QUARTER)
    wo10 = swap(half(w_late, far_columns[0], QUARTER), "z")
    wo_side = swap(half(w_late, far_columns[1], QUARTER), "z")
    wo01 = swap(half(w_out, columns[1], QUARTER), "c")
    wo11 = swap(wo_side, "c")

    attended = kernel_call(
        attend_kernel,
        jax.ShapeDtypeStruct((4, 8, 2, 16, 2 * HD), BF16),
        (place, xa, xb, la, lb, ra, rb, oa, after(ob, wo10), gain, w_rows),
        3 * 10**9,
        9 * 10**6,
        57,
        [
            pltpu.VMEM((2, 8, 32, QUARTER), BF16),
            pltpu.VMEM((512, WIDTH), BF16),
            pltpu.VMEM((WIDTH, 6 * HD), BF16),
            pltpu.VMEM((512, 6 * HD), F32),
            pltpu.SemaphoreType.DMA((2,)),
            pltpu.SemaphoreType.DMA((8,)),
        ],
        left_out=(7, 8, 10),
    )

    attended = lax.all_to_all(attended.reshape(64, 16, 2 * HD), ("x", "y", "z"), 0, 0, tiled=True)
    other = swap(attended, "c")
    shape = (4, 8, 2, 16, 2 * HD)
    mixed = kernel_call(
        output_kernel,
        jax.ShapeDtypeStruct((8, 2, 16, QUARTER), BF16),
        (
            place,
            attended.reshape(shape),
            other.reshape(shape),
            wo00,
            wo10,
            wo01,
            wo11,
            frames_in.reshape(8, 2, 16, QUARTER),
        ),
        8 * 10**8,
        6 * 10**6,
        16,
    )
    return mixed.reshape(1, 1, 256, QUARTER)


def solution(mesh):
    fine = Mesh(mesh.devices.reshape(4, 8, 2, 2, 4), ("x", "y", "z", "c", "dp"))
    seq, tensor = ("x", "y"), ("z", "c")
    in_specs = (P("dp", seq, None, tensor), P(), P(seq, None, tensor), P(tensor, None))
    out_specs = P("dp", seq, None, tensor)
    return jax.shard_map(body, mesh=fine, in_specs=in_specs, out_specs=out_specs, check_vma=False)
```

```python
import jax
import jax.numpy as jnp
from jax import lax
from jax.experimental import pallas as pl
from jax.experimental.pallas import tpu as pltpu
from jax.sharding import Mesh, PartitionSpec as P

HD = 128
WIDTH = 3072
QUARTER = 768
F32 = jnp.float32
BF16 = jnp.bfloat16
VMEM = pl.BlockSpec(memory_space=pltpu.VMEM)
ANY = pl.BlockSpec(memory_space=pl.ANY)
SMEM = pl.BlockSpec(memory_space=pltpu.SMEM)


def ring(size, shift):
    return [(i, (i + shift) % size) for i in range(size)]


def swap(value, axis):
    return lax.ppermute(value, axis, [(0, 1), (1, 0)])


def normalize_block(z, near, far, gain, store):
    parts = []
    for z_far, side in enumerate((near, far)):
        for core in range(2):
            quarter = 2 * lax.rem(z + z_far, 2) + core
            piece = side[:, 16 * core : 16 * core + 16, :].reshape(128, QUARTER).astype(F32)
            parts.append((quarter, piece))
    total = parts[0][1] + parts[1][1] + parts[2][1] + parts[3][1]
    average = jnp.sum(total, axis=-1, keepdims=True) * (1.0 / WIDTH)
    squares = 0.0
    for _, value in parts:
        centred = value - average
        squares = squares + centred * centred
    spread = jnp.sum(squares, axis=-1, keepdims=True) * (1.0 / WIDTH)
    scale = lax.rsqrt(spread + 1e-06)
    for q, value in parts:
        store(q, ((value - average) * scale * gain[q]).astype(BF16))


def attend(projected):
    row = lax.broadcasted_iota(jnp.int32, (256, 256), 0)
    column = lax.broadcasted_iota(jnp.int32, (256, 256), 1)
    same_patch = lax.rem(row, 8) == lax.rem(column, 8)
    heads = []
    for core in range(2):
        groups = []
        for group in range(2):

            def pick(part, core=core, group=group):
                first = (3 * core + part) * HD
                rows = projected[:, first : first + HD].reshape(32, 16, HD)
                return rows[:, 8 * group : 8 * group + 8].reshape(256, HD).astype(BF16)

            query, key, value = pick(0), pick(1), pick(2)
            scores = lax.dot_general(query, key, (((1,), (1,)), ((), ())), preferred_element_type=F32)
            scores = jnp.where(same_patch, scores * HD**-0.5, -jnp.inf)
            weights = jnp.exp(scores - jnp.max(scores, axis=-1, keepdims=True))
            weights = (weights / jnp.sum(weights, axis=-1, keepdims=True)).astype(BF16)
            groups.append(jnp.dot(weights, value, preferred_element_type=F32).reshape(32, 8, HD))
        heads.append(jnp.concatenate(groups, axis=1))
    return jnp.concatenate(heads, axis=2).astype(BF16)


def attend_kernel(place, xa, xb, la, lb, ra, rb, opposite, gain, w_hbm, out, *scratch):
    normed, w_rows, projected, w_sent = scratch
    x, z = place[0], place[1]
    copies = []
    for k in range(4):
        for core in range(2):
            target = w_rows.at[pl.ds(QUARTER * k, QUARTER), pl.ds(3 * HD * core, 3 * HD)]
            source = w_hbm.at[k, pl.ds(QUARTER * core, QUARTER)]
            copies.append(pltpu.make_async_copy(source, target, w_sent.at[2 * k + core]))
    for copy in copies:
        copy.start()
    blocks = ((xa, xb), (la, lb), (ra, rb), (opposite.at[0], opposite.at[1]))
    for i, (near, far) in enumerate(blocks):
        rows = slice(128 * i, 128 * i + 128)

        def store(q, value, rows=rows):
            slot = pl.multiple_of(lax.rem(x + 4 - q, 4) * QUARTER, QUARTER)
            normed[rows, pl.ds(slot, QUARTER)] = value

        normalize_block(z, near, far, gain, store)
    for copy in copies:
        copy.wait()
    for i in range(2):
        rows = slice(256 * i, 256 * i + 256)
        projected[rows] = jnp.dot(normed[rows], w_rows[...], preferred_element_type=F32)
    attended = attend(projected[...])
    for i, shift in enumerate((0, 3, 1, 2)):
        frame = lax.rem(x + shift, 4)
        for chip in range(2):
            out[frame, :, chip] = attended[8 * i : 8 * i + 8]


def output_kernel(place, near, far, wo00, wo10, wo01, wo11, residual, out):
    z, c = place[1], place[2]
    total = jnp.zeros((256, QUARTER), F32)
    for z_far, weights in enumerate(((wo00, wo01), (wo10, wo11))):
        source = lax.rem(z + z_far, 2)
        for c_far, weight in enumerate(weights):
            first = pl.multiple_of(lax.rem(c + c_far, 2) * HD, HD)
            pieces = []
            for half in (near, far):
                columns = [half[s, :, source, :, pl.ds(first, HD)].reshape(128, HD) for s in range(4)]
                pieces.append(jnp.concatenate(columns, axis=1))
            attended = jnp.concatenate(pieces, axis=0)
            total = total + jnp.dot(attended, weight[...], preferred_element_type=F32)
    for half in range(2):
        side = lax.rem(c + half, 2)
        mixed = residual[:, side].astype(F32) + total[128 * half : 128 * half + 128].reshape(8, 16, QUARTER)
        out[:, side] = mixed.astype(BF16)


def slice_kernel(place, source, *outs):
    for k, out in enumerate(outs):
        head = lax.rem(place[0] + k, 4)
        for part in range(3):
            out[:, HD * part : HD * part + HD] = source[part, :, pl.ds(pl.multiple_of(head * HD, HD), HD)]


def after(value, *others):
    return lax.optimization_barrier((value, *others))[0]


def kernel_call(kernel, shapes, operands, flops, moved, mebibytes, scratch=(), left_out=()):
    return pl.pallas_call(
        kernel,
        out_shape=shapes,
        in_specs=[
            SMEM if value.dtype == jnp.int32 else ANY if i in left_out else VMEM
            for i, value in enumerate(operands)
        ],
        out_specs=jax.tree.map(lambda _: VMEM, shapes),
        scratch_shapes=list(scratch),
        compiler_params=pltpu.CompilerParams(vmem_limit_bytes=mebibytes * 2**20),
        cost_estimate=pl.CostEstimate(flops=flops, bytes_accessed=moved, transcendentals=0),
    )(*operands)


def body(frames_in, norm_gain, w_qkv, w_out):
    x, z, c = lax.axis_index("x"), lax.axis_index("z"), lax.axis_index("c")
    place = jnp.stack([x, z, c]).astype(jnp.int32)
    gain = norm_gain.reshape(4, 1, QUARTER)

    slots = kernel_call(
        slice_kernel,
        [jax.ShapeDtypeStruct((96, 3 * HD), BF16)] * 4,
        (place, w_qkv.transpose(1, 0, 2)),
        0,
        6 * 10**5,
        4,
    )
    w_rows = [slots[0]] + [lax.ppermute(slots[k], "x", ring(4, k)) for k in (1, 2, 3)]
    w_rows = jnp.stack(w_rows)

    tokens = frames_in.reshape(16, 16, QUARTER)
    xa = lax.all_to_all(tokens, ("y", "c"), 0, 0, tiled=True).reshape(8, 32, QUARTER)
    xa, w_rows = lax.optimization_barrier((xa, w_rows))
    w_rows = lax.all_gather(w_rows, ("c", "y"), axis=1, tiled=True)
    xb = swap(xa, "z")
    la, ra = (lax.ppermute(xa, "x", ring(4, shift)) for shift in (1, 3))
    xb_late = after(xb, la, ra)
    lb, rb = (lax.ppermute(xb_late, "x", ring(4, shift)) for shift in (1, 3))
    oab = lax.ppermute(jnp.stack([xa, xb_late]), "x", ring(4, 2))

    def half(value, index, size):
        return lax.dynamic_slice_in_dim(value, index * size, size, axis=1)

    wo_keep = half(w_out, z, 2 * QUARTER)
    wo_got = swap(half(after(w_out, xb), 1 - z, 2 * QUARTER), "z")
    wo00, wo10 = half(wo_keep, c, QUARTER), half(wo_got, c, QUARTER)
    wo01, wo11 = swap(half(wo_keep, 1 - c, QUARTER), "c"), swap(half(wo_got, 1 - c, QUARTER), "c")

    attended = kernel_call(
        attend_kernel,
        jax.ShapeDtypeStruct((4, 8, 2, 16, 2 * HD), BF16),
        (place, xa, xb, la, lb, ra, rb, oab, gain, w_rows),
        3 * 10**9,
        9 * 10**6,
        48,
        [
            pltpu.VMEM((512, WIDTH), BF16),
            pltpu.VMEM((WIDTH, 6 * HD), BF16),
            pltpu.VMEM((512, 6 * HD), F32),
            pltpu.SemaphoreType.DMA((8,)),
        ],
        left_out=(9,),
    )

    attended = lax.all_to_all(attended.reshape(64, 16, 2 * HD), ("x", "y", "z"), 0, 0, tiled=True)
    other = swap(attended, "c")
    shape = (4, 8, 2, 16, 2 * HD)
    mixed = kernel_call(
        output_kernel,
        jax.ShapeDtypeStruct((8, 2, 16, QUARTER), BF16),
        (
            place,
            attended.reshape(shape),
            other.reshape(shape),
            wo00,
            wo10,
            wo01,
            wo11,
            frames_in.reshape(8, 2, 16, QUARTER),
        ),
        8 * 10**8,
        6 * 10**6,
        16,
    )
    return mixed.reshape(1, 1, 256, QUARTER)


def solution(mesh):
    fine = Mesh(mesh.devices.reshape(4, 8, 2, 2, 4), ("x", "y", "z", "c", "dp"))
    seq, tensor = ("x", "y"), ("z", "c")
    in_specs = (P("dp", seq, None, tensor), P(), P(seq, None, tensor), P(tensor, None))
    out_specs = P("dp", seq, None, tensor)
    return jax.shard_map(body, mesh=fine, in_specs=in_specs, out_specs=out_specs, check_vma=False)
```

```python
import jax
import jax.numpy as jnp
from jax import lax
from jax.experimental import pallas as pl
from jax.experimental.pallas import tpu as pltpu
from jax.sharding import Mesh, PartitionSpec as P

HD = 128
WIDTH = 3072
QUARTER = 768
F32 = jnp.float32
BF16 = jnp.bfloat16
VMEM = pl.BlockSpec(memory_space=pltpu.VMEM)
ANY = pl.BlockSpec(memory_space=pl.ANY)
SMEM = pl.BlockSpec(memory_space=pltpu.SMEM)


def ring(size, shift):
    return [(i, (i + shift) % size) for i in range(size)]


def across():
    pairs = []
    for i in range(4):
        pairs.append((2 * i, 2 * ((i + 1) % 4)))
        pairs.append((2 * i + 1, 2 * ((i + 3) % 4) + 1))
    return pairs


def swap(value, axis):
    return lax.ppermute(value, axis, [(0, 1), (1, 0)])


def normalize_block(z, near, far, gain, store):
    parts = []
    for z_far, side in enumerate((near, far)):
        for core in range(2):
            quarter = 2 * lax.rem(z + z_far, 2) + core
            piece = side[:, 16 * core : 16 * core + 16, :].reshape(128, QUARTER).astype(F32)
            parts.append((quarter, piece))
    total = parts[0][1] + parts[1][1] + parts[2][1] + parts[3][1]
    average = jnp.sum(total, axis=-1, keepdims=True) * (1.0 / WIDTH)
    squares = 0.0
    for _, value in parts:
        centred = value - average
        squares = squares + centred * centred
    spread = jnp.sum(squares, axis=-1, keepdims=True) * (1.0 / WIDTH)
    scale = lax.rsqrt(spread + 1e-06)
    for q, value in parts:
        store(q, ((value - average) * scale * gain[q]).astype(BF16))


def attend(projected):
    row = lax.broadcasted_iota(jnp.int32, (256, 256), 0)
    column = lax.broadcasted_iota(jnp.int32, (256, 256), 1)
    same_patch = lax.rem(row, 8) == lax.rem(column, 8)
    heads = []
    for core in range(2):
        groups = []
        for group in range(2):

            def pick(part, core=core, group=group):
                first = (3 * core + part) * HD
                rows = projected[:, first : first + HD].reshape(32, 16, HD)
                return rows[:, 8 * group : 8 * group + 8].reshape(256, HD).astype(BF16)

            query, key, value = pick(0), pick(1), pick(2)
            scores = lax.dot_general(query, key, (((1,), (1,)), ((), ())), preferred_element_type=F32)
            scores = jnp.where(same_patch, scores * HD**-0.5, -jnp.inf)
            weights = jnp.exp(scores - jnp.max(scores, axis=-1, keepdims=True))
            weights = (weights / jnp.sum(weights, axis=-1, keepdims=True)).astype(BF16)
            groups.append(jnp.dot(weights, value, preferred_element_type=F32).reshape(32, 8, HD))
        heads.append(jnp.concatenate(groups, axis=1))
    return jnp.concatenate(heads, axis=2).astype(BF16)


def attend_kernel(place, xa, xb, la, lb, ra, rb, oa, ob, gain, w_hbm, out, *scratch):
    normed, w_rows, projected, w_sent = scratch
    x, z = place[0], place[1]
    copies = []
    for k in range(4):
        for core in range(2):
            target = w_rows.at[pl.ds(QUARTER * k, QUARTER), pl.ds(3 * HD * core, 3 * HD)]
            source = w_hbm.at[k, pl.ds(QUARTER * core, QUARTER)]
            copies.append(pltpu.make_async_copy(source, target, w_sent.at[2 * k + core]))
    for copy in copies:
        copy.start()
    blocks = ((xa, xb), (la, lb), (ra, rb), (oa, ob))
    for i, (near, far) in enumerate(blocks):
        rows = slice(128 * i, 128 * i + 128)

        def store(q, value, rows=rows):
            slot = pl.multiple_of(lax.rem(x + 4 - q, 4) * QUARTER, QUARTER)
            normed[rows, pl.ds(slot, QUARTER)] = value

        normalize_block(z, near, far, gain, store)
    for copy in copies:
        copy.wait()
    for i in range(2):
        rows = slice(256 * i, 256 * i + 256)
        projected[rows] = jnp.dot(normed[rows], w_rows[...], preferred_element_type=F32)
    attended = attend(projected[...])
    for i, shift in enumerate((0, 3, 1, 2)):
        frame = lax.rem(x + shift, 4)
        for chip in range(2):
            out[frame, :, chip] = attended[8 * i : 8 * i + 8]


def output_kernel(place, near, far, wo00, wo10, wo01, wo11, residual, out):
    z, c = place[1], place[2]
    total = jnp.zeros((256, QUARTER), F32)
    for z_far, weights in enumerate(((wo00, wo01), (wo10, wo11))):
        source = lax.rem(z + z_far, 2)
        for c_far, weight in enumerate(weights):
            first = pl.multiple_of(lax.rem(c + c_far, 2) * HD, HD)
            pieces = []
            for half in (near, far):
                columns = [half[s, :, source, :, pl.ds(first, HD)].reshape(128, HD) for s in range(4)]
                pieces.append(jnp.concatenate(columns, axis=1))
            attended = jnp.concatenate(pieces, axis=0)
            total = total + jnp.dot(attended, weight[...], preferred_element_type=F32)
    for half in range(2):
        side = lax.rem(c + half, 2)
        mixed = residual[:, side].astype(F32) + total[128 * half : 128 * half + 128].reshape(8, 16, QUARTER)
        out[:, side] = mixed.astype(BF16)


def slice_kernel(place, source, *outs):
    for k, out in enumerate(outs):
        head = lax.rem(place[0] + k, 4)
        for part in range(3):
            out[:, HD * part : HD * part + HD] = source[part, :, pl.ds(pl.multiple_of(head * HD, HD), HD)]


def after(value, *others):
    return lax.optimization_barrier((value, *others))[0]


def kernel_call(kernel, shapes, operands, flops, moved, mebibytes, scratch=(), left_out=()):
    return pl.pallas_call(
        kernel,
        out_shape=shapes,
        in_specs=[
            SMEM if value.dtype == jnp.int32 else ANY if i in left_out else VMEM
            for i, value in enumerate(operands)
        ],
        out_specs=jax.tree.map(lambda _: VMEM, shapes),
        scratch_shapes=list(scratch),
        compiler_params=pltpu.CompilerParams(vmem_limit_bytes=mebibytes * 2**20),
        cost_estimate=pl.CostEstimate(flops=flops, bytes_accessed=moved, transcendentals=0),
    )(*operands)


def body(frames_in, norm_gain, w_qkv, w_out):
    x, z, c = lax.axis_index("x"), lax.axis_index("z"), lax.axis_index("c")
    place = jnp.stack([x, z, c]).astype(jnp.int32)
    gain = norm_gain.reshape(4, 1, QUARTER)

    slots = kernel_call(
        slice_kernel,
        [jax.ShapeDtypeStruct((96, 3 * HD), BF16)] * 4,
        (place, w_qkv.transpose(1, 0, 2)),
        0,
        6 * 10**5,
        4,
    )
    w_rows = [slots[0]] + [lax.ppermute(slots[k], "x", ring(4, k)) for k in (1, 2, 3)]
    w_rows = jnp.stack(w_rows)

    tokens = frames_in.reshape(16, 16, QUARTER)
    xa = lax.all_to_all(tokens, ("y", "c"), 0, 0, tiled=True).reshape(8, 32, QUARTER)
    xa, w_rows = lax.optimization_barrier((xa, w_rows))
    w_rows = lax.all_gather(w_rows, ("c", "y"), axis=1, tiled=True)
    xb = swap(xa, "z")
    la, ra = (lax.ppermute(xa, "x", ring(4, shift)) for shift in (1, 3))
    xb_late = after(xb, la, ra)
    lb, rb = (lax.ppermute(xb_late, "x", ring(4, shift)) for shift in (1, 3))
    oa = lax.ppermute(jnp.where(c == 0, la, ra), ("x", "c"), across())
    ob = lax.ppermute(jnp.where(c == 0, lb, rb), ("x", "c"), across())

    def half(value, index, size):
        return lax.dynamic_slice_in_dim(value, index * size, size, axis=1)

    wo_keep = half(w_out, z, 2 * QUARTER)
    wo_got = swap(half(after(w_out, xb), 1 - z, 2 * QUARTER), "z")
    wo00, wo10 = half(wo_keep, c, QUARTER), half(wo_got, c, QUARTER)
    wo01, wo11 = swap(half(wo_keep, 1 - c, QUARTER), "c"), swap(half(wo_got, 1 - c, QUARTER), "c")

    attended = kernel_call(
        attend_kernel,
        jax.ShapeDtypeStruct((4, 8, 2, 16, 2 * HD), BF16),
        (place, xa, xb, la, lb, ra, rb, oa, ob, gain, w_rows),
        3 * 10**9,
        9 * 10**6,
        48,
        [
            pltpu.VMEM((512, WIDTH), BF16),
            pltpu.VMEM((WIDTH, 6 * HD), BF16),
            pltpu.VMEM((512, 6 * HD), F32),
            pltpu.SemaphoreType.DMA((8,)),
        ],
        left_out=(10,),
    )

    attended = lax.all_to_all(attended.reshape(64, 16, 2 * HD), ("x", "y", "z"), 0, 0, tiled=True)
    other = swap(attended, "c")
    shape = (4, 8, 2, 16, 2 * HD)
    mixed = kernel_call(
        output_kernel,
        jax.ShapeDtypeStruct((8, 2, 16, QUARTER), BF16),
        (
            place,
            attended.reshape(shape),
            other.reshape(shape),
            wo00,
            wo10,
            wo01,
            wo11,
            frames_in.reshape(8, 2, 16, QUARTER),
        ),
        8 * 10**8,
        6 * 10**6,
        16,
    )
    return mixed.reshape(1, 1, 256, QUARTER)


def solution(mesh):
    fine = Mesh(mesh.devices.reshape(4, 8, 2, 2, 4), ("x", "y", "z", "c", "dp"))
    seq, tensor = ("x", "y"), ("z", "c")
    in_specs = (P("dp", seq, None, tensor), P(), P(seq, None, tensor), P(tensor, None))
    out_specs = P("dp", seq, None, tensor)
    return jax.shard_map(body, mesh=fine, in_specs=in_specs, out_specs=out_specs, check_vma=False)
```

```python
import jax
import jax.numpy as jnp
from jax import lax
from jax.experimental import pallas as pl
from jax.experimental.pallas import tpu as pltpu
from jax.sharding import Mesh, PartitionSpec as P

HD = 128
WIDTH = 3072
QUARTER = 768
F32 = jnp.float32
BF16 = jnp.bfloat16
VMEM = pl.BlockSpec(memory_space=pltpu.VMEM)
ANY = pl.BlockSpec(memory_space=pl.ANY)
SMEM = pl.BlockSpec(memory_space=pltpu.SMEM)


def ring(size, shift):
    return [(i, (i + shift) % size) for i in range(size)]


def across():
    pairs = []
    for i in range(4):
        pairs.append((2 * i, 2 * ((i + 1) % 4)))
        pairs.append((2 * i + 1, 2 * ((i + 3) % 4) + 1))
    return pairs


def swap(value, axis):
    return lax.ppermute(value, axis, [(0, 1), (1, 0)])


def normalize_block(z, near, far, gain, store):
    parts = []
    for z_far, side in enumerate((near, far)):
        for core in range(2):
            quarter = 2 * lax.rem(z + z_far, 2) + core
            piece = side[:, 16 * core : 16 * core + 16, :].reshape(128, QUARTER).astype(F32)
            parts.append((quarter, piece))
    total = parts[0][1] + parts[1][1] + parts[2][1] + parts[3][1]
    average = jnp.sum(total, axis=-1, keepdims=True) * (1.0 / WIDTH)
    squares = 0.0
    for _, value in parts:
        centred = value - average
        squares = squares + centred * centred
    spread = jnp.sum(squares, axis=-1, keepdims=True) * (1.0 / WIDTH)
    scale = lax.rsqrt(spread + 1e-06)
    for q, value in parts:
        store(q, ((value - average) * scale * gain[q]).astype(BF16))


def attend(projected):
    row = lax.broadcasted_iota(jnp.int32, (256, 256), 0)
    column = lax.broadcasted_iota(jnp.int32, (256, 256), 1)
    same_patch = lax.rem(row, 8) == lax.rem(column, 8)
    heads = []
    for core in range(2):
        groups = []
        for group in range(2):

            def pick(part, core=core, group=group):
                first = (3 * core + part) * HD
                rows = projected[:, first : first + HD].reshape(32, 16, HD)
                return rows[:, 8 * group : 8 * group + 8].reshape(256, HD).astype(BF16)

            query, key, value = pick(0), pick(1), pick(2)
            scores = lax.dot_general(query, key, (((1,), (1,)), ((), ())), preferred_element_type=F32)
            scores = jnp.where(same_patch, scores * HD**-0.5, -jnp.inf)
            weights = jnp.exp(scores - jnp.max(scores, axis=-1, keepdims=True))
            weights = (weights / jnp.sum(weights, axis=-1, keepdims=True)).astype(BF16)
            groups.append(jnp.dot(weights, value, preferred_element_type=F32).reshape(32, 8, HD))
        heads.append(jnp.concatenate(groups, axis=1))
    return jnp.concatenate(heads, axis=2).astype(BF16)


def attend_kernel(place, xa, xb, la, lb, ra, rb, oa, ob, gain, w_hbm, out, *scratch):
    normed, w_rows, projected, w_sent = scratch
    x, z = place[0], place[1]
    copies = []
    for k in range(4):
        for core in range(2):
            target = w_rows.at[pl.ds(QUARTER * k, QUARTER), pl.ds(3 * HD * core, 3 * HD)]
            source = w_hbm.at[k, pl.ds(QUARTER * core, QUARTER)]
            copies.append(pltpu.make_async_copy(source, target, w_sent.at[2 * k + core]))
    for copy in copies:
        copy.start()
    blocks = ((xa, xb), (la, lb), (ra, rb), (oa, ob))
    for i, (near, far) in enumerate(blocks):
        rows = slice(128 * i, 128 * i + 128)

        def store(q, value, rows=rows):
            slot = pl.multiple_of(lax.rem(x + 4 - q, 4) * QUARTER, QUARTER)
            normed[rows, pl.ds(slot, QUARTER)] = value

        normalize_block(z, near, far, gain, store)
    for copy in copies:
        copy.wait()
    for i in range(2):
        rows = slice(256 * i, 256 * i + 256)
        projected[rows] = jnp.dot(normed[rows], w_rows[...], preferred_element_type=F32)
    attended = attend(projected[...])
    for i, shift in enumerate((0, 3, 1, 2)):
        frame = lax.rem(x + shift, 4)
        for chip in range(2):
            out[frame, :, chip] = attended[8 * i : 8 * i + 8]


def output_kernel(place, near, far, wo00, wo10, wo01, wo11, residual, out):
    z, c = place[1], place[2]
    total = jnp.zeros((256, QUARTER), F32)
    for z_far, weights in enumerate(((wo00, wo01), (wo10, wo11))):
        source = lax.rem(z + z_far, 2)
        for c_far, weight in enumerate(weights):
            first = pl.multiple_of(lax.rem(c + c_far, 2) * HD, HD)
            pieces = []
            for half in (near, far):
                columns = [half[s, :, source, :, pl.ds(first, HD)].reshape(128, HD) for s in range(4)]
                pieces.append(jnp.concatenate(columns, axis=1))
            attended = jnp.concatenate(pieces, axis=0)
            total = total + jnp.dot(attended, weight[...], preferred_element_type=F32)
    for half in range(2):
        side = lax.rem(c + half, 2)
        mixed = residual[:, side].astype(F32) + total[128 * half : 128 * half + 128].reshape(8, 16, QUARTER)
        out[:, side] = mixed.astype(BF16)


def slice_kernel(place, source, *refs):
    outs, sent = refs[:4], refs[4]
    copies = []
    for k, out in enumerate(outs):
        head = pl.multiple_of(lax.rem(place[0] + k, 4) * HD, HD)
        for part in range(3):
            target = out.at[:, pl.ds(HD * part, HD)]
            copies.append(pltpu.make_async_copy(source.at[part, :, pl.ds(head, HD)], target, sent.at[3 * k + part]))
    for copy in copies:
        copy.start()
    for copy in copies:
        copy.wait()


def after(value, *others):
    return lax.optimization_barrier((value, *others))[0]


def kernel_call(kernel, shapes, operands, flops, moved, mebibytes, scratch=(), left_out=()):
    return pl.pallas_call(
        kernel,
        out_shape=shapes,
        in_specs=[
            SMEM if value.dtype == jnp.int32 else ANY if i in left_out else VMEM
            for i, value in enumerate(operands)
        ],
        out_specs=jax.tree.map(lambda _: VMEM, shapes),
        scratch_shapes=list(scratch),
        compiler_params=pltpu.CompilerParams(vmem_limit_bytes=mebibytes * 2**20),
        cost_estimate=pl.CostEstimate(flops=flops, bytes_accessed=moved, transcendentals=0),
    )(*operands)


def body(frames_in, norm_gain, w_qkv, w_out):
    x, z, c = lax.axis_index("x"), lax.axis_index("z"), lax.axis_index("c")
    place = jnp.stack([x, z, c]).astype(jnp.int32)
    gain = norm_gain.reshape(4, 1, QUARTER)

    slots = kernel_call(
        slice_kernel,
        [jax.ShapeDtypeStruct((96, 3 * HD), BF16)] * 4,
        (place, w_qkv.transpose(1, 0, 2)),
        0,
        6 * 10**5,
        4,
        [pltpu.SemaphoreType.DMA((12,))],
        left_out=(1,),
    )
    w_rows = [slots[0]] + [lax.ppermute(slots[k], "x", ring(4, k)) for k in (1, 2, 3)]
    w_rows = jnp.stack(w_rows)

    tokens = frames_in.reshape(16, 16, QUARTER)
    xa = lax.all_to_all(tokens, ("y", "c"), 0, 0, tiled=True).reshape(8, 32, QUARTER)
    xa, w_rows = lax.optimization_barrier((xa, w_rows))
    w_rows = lax.all_gather(w_rows, ("c", "y"), axis=1, tiled=True)
    xb = swap(xa, "z")
    la, ra = (lax.ppermute(xa, "x", ring(4, shift)) for shift in (1, 3))
    xb_late = after(xb, la)
    lb, rb = (lax.ppermute(xb_late, "x", ring(4, shift)) for shift in (1, 3))
    oa = lax.ppermute(jnp.where(c == 0, la, ra), ("x", "c"), across())
    ob = lax.ppermute(jnp.where(c == 0, lb, rb), ("x", "c"), across())

    def half(value, index, size):
        return lax.dynamic_slice_in_dim(value, index * size, size, axis=1)

    wo_keep = half(w_out, z, 2 * QUARTER)
    wo_got = swap(half(after(w_out, xb), 1 - z, 2 * QUARTER), "z")
    wo00, wo10 = half(wo_keep, c, QUARTER), half(wo_got, c, QUARTER)
    wo01, wo11 = swap(half(wo_keep, 1 - c, QUARTER), "c"), swap(half(wo_got, 1 - c, QUARTER), "c")

    attended = kernel_call(
        attend_kernel,
        jax.ShapeDtypeStruct((4, 8, 2, 16, 2 * HD), BF16),
        (place, xa, xb, la, lb, ra, rb, oa, ob, gain, w_rows),
        3 * 10**9,
        9 * 10**6,
        48,
        [
            pltpu.VMEM((512, WIDTH), BF16),
            pltpu.VMEM((WIDTH, 6 * HD), BF16),
            pltpu.VMEM((512, 6 * HD), F32),
            pltpu.SemaphoreType.DMA((8,)),
        ],
        left_out=(10,),
    )

    attended = lax.all_to_all(attended.reshape(64, 16, 2 * HD), ("x", "y", "z"), 0, 0, tiled=True)
    other = swap(attended, "c")
    shape = (4, 8, 2, 16, 2 * HD)
    mixed = kernel_call(
        output_kernel,
        jax.ShapeDtypeStruct((8, 2, 16, QUARTER), BF16),
        (
            place,
            attended.reshape(shape),
            other.reshape(shape),
            wo00,
            wo10,
            wo01,
            wo11,
            frames_in.reshape(8, 2, 16, QUARTER),
        ),
        8 * 10**8,
        6 * 10**6,
        16,
    )
    return mixed.reshape(1, 1, 256, QUARTER)


def solution(mesh):
    fine = Mesh(mesh.devices.reshape(4, 8, 2, 2, 4), ("x", "y", "z", "c", "dp"))
    seq, tensor = ("x", "y"), ("z", "c")
    in_specs = (P("dp", seq, None, tensor), P(), P(seq, None, tensor), P(tensor, None))
    out_specs = P("dp", seq, None, tensor)
    return jax.shard_map(body, mesh=fine, in_specs=in_specs, out_specs=out_specs, check_vma=False)
```

```python
import jax
import jax.numpy as jnp
from jax import lax
from jax.experimental import pallas as pl
from jax.experimental.pallas import tpu as pltpu
from jax.sharding import Mesh, PartitionSpec as P

HD = 128
WIDTH = 3072
QUARTER = 768
F32 = jnp.float32
BF16 = jnp.bfloat16
VMEM = pl.BlockSpec(memory_space=pltpu.VMEM)
ANY = pl.BlockSpec(memory_space=pl.ANY)
SMEM = pl.BlockSpec(memory_space=pltpu.SMEM)


def ring(size, shift):
    return [(i, (i + shift) % size) for i in range(size)]


def across():
    pairs = []
    for i in range(4):
        pairs.append((2 * i, 2 * ((i + 1) % 4)))
        pairs.append((2 * i + 1, 2 * ((i + 3) % 4) + 1))
    return pairs


def swap(value, axis):
    return lax.ppermute(value, axis, [(0, 1), (1, 0)])


def normalize_block(z, near, far, gain, store):
    parts = []
    for z_far, side in enumerate((near, far)):
        for core in range(2):
            quarter = 2 * lax.rem(z + z_far, 2) + core
            piece = side[:, 16 * core : 16 * core + 16, :].reshape(128, QUARTER).astype(F32)
            parts.append((quarter, piece))
    total = parts[0][1] + parts[1][1] + parts[2][1] + parts[3][1]
    average = jnp.sum(total, axis=-1, keepdims=True) * (1.0 / WIDTH)
    squares = 0.0
    for _, value in parts:
        centred = value - average
        squares = squares + centred * centred
    spread = jnp.sum(squares, axis=-1, keepdims=True) * (1.0 / WIDTH)
    scale = lax.rsqrt(spread + 1e-06)
    for q, value in parts:
        store(q, ((value - average) * scale * gain[q]).astype(BF16))


def attend(projected):
    row = lax.broadcasted_iota(jnp.int32, (256, 256), 0)
    column = lax.broadcasted_iota(jnp.int32, (256, 256), 1)
    same_patch = lax.rem(row, 8) == lax.rem(column, 8)
    heads = []
    for core in range(2):
        groups = []
        for group in range(2):

            def pick(part, core=core, group=group):
                first = (3 * core + part) * HD
                rows = projected[:, first : first + HD].reshape(32, 16, HD)
                return rows[:, 8 * group : 8 * group + 8].reshape(256, HD).astype(BF16)

            query, key, value = pick(0), pick(1), pick(2)
            scores = lax.dot_general(query, key, (((1,), (1,)), ((), ())), preferred_element_type=F32)
            scores = jnp.where(same_patch, scores * HD**-0.5, -jnp.inf)
            weights = jnp.exp(scores - jnp.max(scores, axis=-1, keepdims=True))
            weights = (weights / jnp.sum(weights, axis=-1, keepdims=True)).astype(BF16)
            groups.append(jnp.dot(weights, value, preferred_element_type=F32).reshape(32, 8, HD))
        heads.append(jnp.concatenate(groups, axis=1))
    return jnp.concatenate(heads, axis=2).astype(BF16)


def attend_kernel(place, xa, xb, la, lb, ra, rb, oa, ob, gain, w_hbm, out, *scratch):
    normed, w_rows, projected, w_sent = scratch
    x, z = place[0], place[1]
    copies = []
    for k in range(4):
        for core in range(2):
            target = w_rows.at[k, :, :, pl.ds(3 * HD * core, 3 * HD)]
            source = w_hbm.at[pl.ds(8 * core, 8), k]
            copies.append(pltpu.make_async_copy(source, target, w_sent.at[2 * k + core]))
    for copy in copies:
        copy.start()
    blocks = ((xa, xb), (la, lb), (ra, rb), (oa, ob))
    for i, (near, far) in enumerate(blocks):
        rows = slice(128 * i, 128 * i + 128)

        def store(q, value, rows=rows):
            slot = pl.multiple_of(lax.rem(x + 4 - q, 4) * QUARTER, QUARTER)
            normed[rows, pl.ds(slot, QUARTER)] = value

        normalize_block(z, near, far, gain, store)
    for copy in copies:
        copy.wait()
    for i in range(2):
        rows = slice(256 * i, 256 * i + 256)
        projected[rows] = jnp.dot(normed[rows], w_rows[...].reshape(WIDTH, 6 * HD), preferred_element_type=F32)
    attended = attend(projected[...])
    for i, shift in enumerate((0, 3, 1, 2)):
        frame = lax.rem(x + shift, 4)
        for chip in range(2):
            out[frame, :, chip] = attended[8 * i : 8 * i + 8]


def output_kernel(place, near, far, wo00, wo10, wo01, wo11, residual, out):
    z, c = place[1], place[2]
    total = jnp.zeros((256, QUARTER), F32)
    for z_far, weights in enumerate(((wo00, wo01), (wo10, wo11))):
        source = lax.rem(z + z_far, 2)
        for c_far, weight in enumerate(weights):
            first = pl.multiple_of(lax.rem(c + c_far, 2) * HD, HD)
            pieces = []
            for half in (near, far):
                columns = [half[s, :, source, :, pl.ds(first, HD)].reshape(128, HD) for s in range(4)]
                pieces.append(jnp.concatenate(columns, axis=1))
            attended = jnp.concatenate(pieces, axis=0)
            total = total + jnp.dot(attended, weight[...], preferred_element_type=F32)
    for half in range(2):
        side = lax.rem(c + half, 2)
        mixed = residual[:, side].astype(F32) + total[128 * half : 128 * half + 128].reshape(8, 16, QUARTER)
        out[:, side] = mixed.astype(BF16)


def slice_kernel(place, source, *outs):
    for k, out in enumerate(outs):
        head = lax.rem(place[0] + k, 4)
        for part in range(3):
            out[:, HD * part : HD * part + HD] = source[part, :, pl.ds(pl.multiple_of(head * HD, HD), HD)]


def after(value, *others):
    return lax.optimization_barrier((value, *others))[0]


def kernel_call(kernel, shapes, operands, flops, moved, mebibytes, scratch=(), left_out=()):
    return pl.pallas_call(
        kernel,
        out_shape=shapes,
        in_specs=[
            SMEM if value.dtype == jnp.int32 else ANY if i in left_out else VMEM
            for i, value in enumerate(operands)
        ],
        out_specs=jax.tree.map(lambda _: VMEM, shapes),
        scratch_shapes=list(scratch),
        compiler_params=pltpu.CompilerParams(vmem_limit_bytes=mebibytes * 2**20),
        cost_estimate=pl.CostEstimate(flops=flops, bytes_accessed=moved, transcendentals=0),
    )(*operands)


def body(frames_in, norm_gain, w_qkv, w_out):
    x, z, c = lax.axis_index("x"), lax.axis_index("z"), lax.axis_index("c")
    place = jnp.stack([x, z, c]).astype(jnp.int32)
    gain = norm_gain.reshape(4, 1, QUARTER)

    slots = kernel_call(
        slice_kernel,
        [jax.ShapeDtypeStruct((96, 3 * HD), BF16)] * 4,
        (place, w_qkv.transpose(1, 0, 2)),
        0,
        6 * 10**5,
        4,
    )
    w_rows = [slots[0]] + [lax.ppermute(slots[k], "x", ring(4, k)) for k in (1, 2, 3)]
    w_rows = jnp.stack(w_rows)

    tokens = frames_in.reshape(16, 16, QUARTER)
    xa = lax.all_to_all(tokens, ("y", "c"), 0, 0, tiled=True).reshape(8, 32, QUARTER)
    xa, w_rows = lax.optimization_barrier((xa, w_rows))
    w_rows = lax.all_gather(w_rows, ("c", "y"))
    xb = swap(xa, "z")
    la, ra = (lax.ppermute(xa, "x", ring(4, shift)) for shift in (1, 3))
    xb_late = after(xb, la, ra)
    lb, rb = (lax.ppermute(xb_late, "x", ring(4, shift)) for shift in (1, 3))
    oa = lax.ppermute(jnp.where(c == 0, la, ra), ("x", "c"), across())
    ob = lax.ppermute(jnp.where(c == 0, lb, rb), ("x", "c"), across())

    def half(value, index, size):
        return lax.dynamic_slice_in_dim(value, index * size, size, axis=1)

    wo_keep = half(w_out, z, 2 * QUARTER)
    wo_got = swap(half(after(w_out, xb), 1 - z, 2 * QUARTER), "z")
    wo00, wo10 = half(wo_keep, c, QUARTER), half(wo_got, c, QUARTER)
    wo01, wo11 = swap(half(wo_keep, 1 - c, QUARTER), "c"), swap(half(wo_got, 1 - c, QUARTER), "c")

    attended = kernel_call(
        attend_kernel,
        jax.ShapeDtypeStruct((4, 8, 2, 16, 2 * HD), BF16),
        (place, xa, xb, la, lb, ra, rb, oa, ob, gain, w_rows),
        3 * 10**9,
        9 * 10**6,
        48,
        [
            pltpu.VMEM((512, WIDTH), BF16),
            pltpu.VMEM((4, 8, 96, 6 * HD), BF16),
            pltpu.VMEM((512, 6 * HD), F32),
            pltpu.SemaphoreType.DMA((8,)),
        ],
        left_out=(10,),
    )

    attended = lax.all_to_all(attended.reshape(64, 16, 2 * HD), ("x", "y", "z"), 0, 0, tiled=True)
    other = swap(attended, "c")
    shape = (4, 8, 2, 16, 2 * HD)
    mixed = kernel_call(
        output_kernel,
        jax.ShapeDtypeStruct((8, 2, 16, QUARTER), BF16),
        (
            place,
            attended.reshape(shape),
            other.reshape(shape),
            wo00,
            wo10,
            wo01,
            wo11,
            frames_in.reshape(8, 2, 16, QUARTER),
        ),
        8 * 10**8,
        6 * 10**6,
        16,
    )
    return mixed.reshape(1, 1, 256, QUARTER)


def solution(mesh):
    fine = Mesh(mesh.devices.reshape(4, 8, 2, 2, 4), ("x", "y", "z", "c", "dp"))
    seq, tensor = ("x", "y"), ("z", "c")
    in_specs = (P("dp", seq, None, tensor), P(), P(seq, None, tensor), P(tensor, None))
    out_specs = P("dp", seq, None, tensor)
    return jax.shard_map(body, mesh=fine, in_specs=in_specs, out_specs=out_specs, check_vma=False)
```

```python
import jax
import jax.numpy as jnp
from jax import lax
from jax.experimental import pallas as pl
from jax.experimental.pallas import tpu as pltpu
from jax.sharding import Mesh, PartitionSpec as P

HD = 128
WIDTH = 3072
QUARTER = 768
F32 = jnp.float32
BF16 = jnp.bfloat16
VMEM = pl.BlockSpec(memory_space=pltpu.VMEM)
ANY = pl.BlockSpec(memory_space=pl.ANY)
SMEM = pl.BlockSpec(memory_space=pltpu.SMEM)


def ring(size, shift):
    return [(i, (i + shift) % size) for i in range(size)]


def across():
    pairs = []
    for i in range(4):
        pairs.append((2 * i, 2 * ((i + 1) % 4)))
        pairs.append((2 * i + 1, 2 * ((i + 3) % 4) + 1))
    return pairs


def swap(value, axis):
    return lax.ppermute(value, axis, [(0, 1), (1, 0)])


def normalize_block(z, near, far, gain, store):
    parts = []
    for z_far, side in enumerate((near, far)):
        for core in range(2):
            quarter = 2 * lax.rem(z + z_far, 2) + core
            piece = side[:, 16 * core : 16 * core + 16, :].reshape(128, QUARTER).astype(F32)
            parts.append((quarter, piece))
    total = parts[0][1] + parts[1][1] + parts[2][1] + parts[3][1]
    average = jnp.sum(total, axis=-1, keepdims=True) * (1.0 / WIDTH)
    squares = 0.0
    for _, value in parts:
        centred = value - average
        squares = squares + centred * centred
    spread = jnp.sum(squares, axis=-1, keepdims=True) * (1.0 / WIDTH)
    scale = lax.rsqrt(spread + 1e-06)
    for q, value in parts:
        store(q, ((value - average) * scale * gain[q]).astype(BF16))


def attend(projected):
    row = lax.broadcasted_iota(jnp.int32, (256, 256), 0)
    column = lax.broadcasted_iota(jnp.int32, (256, 256), 1)
    same_patch = lax.rem(row, 8) == lax.rem(column, 8)
    heads = []
    for core in range(2):
        groups = []
        for group in range(2):

            def pick(part, core=core, group=group):
                first = (3 * core + part) * HD
                rows = projected[:, first : first + HD].reshape(32, 16, HD)
                return rows[:, 8 * group : 8 * group + 8].reshape(256, HD).astype(BF16)

            query, key, value = pick(0), pick(1), pick(2)
            scores = lax.dot_general(query, key, (((1,), (1,)), ((), ())), preferred_element_type=F32)
            scores = jnp.where(same_patch, scores * HD**-0.5, -jnp.inf)
            weights = jnp.exp(scores - jnp.max(scores, axis=-1, keepdims=True))
            weights = (weights / jnp.sum(weights, axis=-1, keepdims=True)).astype(BF16)
            groups.append(jnp.dot(weights, value, preferred_element_type=F32).reshape(32, 8, HD))
        heads.append(jnp.concatenate(groups, axis=1))
    return jnp.concatenate(heads, axis=2).astype(BF16)


def attend_kernel(place, xa, xb, la, lb, ra, rb, oa, ob, gain, w_hbm, out, *scratch):
    normed, w_rows, projected, w_sent = scratch
    x, z = place[0], place[1]
    copies = []
    for k in range(4):
        for core in range(2):
            target = w_rows.at[pl.ds(QUARTER * k, QUARTER), pl.ds(3 * HD * core, 3 * HD)]
            source = w_hbm.at[k, pl.ds(QUARTER * core, QUARTER)]
            copies.append(pltpu.make_async_copy(source, target, w_sent.at[2 * k + core]))
    for copy in copies:
        copy.start()
    blocks = ((xa, xb), (la, lb), (ra, rb), (oa, ob))
    for i, (near, far) in enumerate(blocks):
        rows = slice(128 * i, 128 * i + 128)

        def store(q, value, rows=rows):
            slot = pl.multiple_of(lax.rem(x + 4 - q, 4) * QUARTER, QUARTER)
            normed[rows, pl.ds(slot, QUARTER)] = value

        normalize_block(z, near, far, gain, store)
    for copy in copies:
        copy.wait()
    for i in range(2):
        rows = slice(256 * i, 256 * i + 256)
        projected[rows] = jnp.dot(normed[rows], w_rows[...], preferred_element_type=F32)
    attended = attend(projected[...])
    for i, shift in enumerate((0, 3, 1, 2)):
        frame = lax.rem(x + shift, 4)
        for chip in range(2):
            out[frame, :, chip] = attended[8 * i : 8 * i + 8]


def output_kernel(place, near, far, wo00, wo10, wo01, wo11, residual, out):
    z, c = place[1], place[2]
    total = jnp.zeros((256, QUARTER), F32)
    for z_far, weights in enumerate(((wo00, wo01), (wo10, wo11))):
        source = lax.rem(z + z_far, 2)
        for c_far, weight in enumerate(weights):
            first = pl.multiple_of(lax.rem(c + c_far, 2) * HD, HD)
            pieces = []
            for half in (near, far):
                columns = [half[s, :, source, :, pl.ds(first, HD)].reshape(128, HD) for s in range(4)]
                pieces.append(jnp.concatenate(columns, axis=1))
            attended = jnp.concatenate(pieces, axis=0)
            total = total + jnp.dot(attended, weight[...], preferred_element_type=F32)
    for half in range(2):
        side = lax.rem(c + half, 2)
        mixed = residual[:, side].astype(F32) + total[128 * half : 128 * half + 128].reshape(8, 16, QUARTER)
        out[:, side] = mixed.astype(BF16)


def slice_kernel(place, source, *outs):
    for k, out in enumerate(outs):
        head = lax.rem(place[0] + k, 4)
        for part in range(3):
            out[:, HD * part : HD * part + HD] = source[part, :, pl.ds(pl.multiple_of(head * HD, HD), HD)]


def after(value, *others):
    return lax.optimization_barrier((value, *others))[0]


def kernel_call(kernel, shapes, operands, flops, moved, mebibytes, scratch=(), left_out=()):
    return pl.pallas_call(
        kernel,
        out_shape=shapes,
        in_specs=[
            SMEM if value.dtype == jnp.int32 else ANY if i in left_out else VMEM
            for i, value in enumerate(operands)
        ],
        out_specs=jax.tree.map(lambda _: VMEM, shapes),
        scratch_shapes=list(scratch),
        compiler_params=pltpu.CompilerParams(vmem_limit_bytes=mebibytes * 2**20),
        cost_estimate=pl.CostEstimate(flops=flops, bytes_accessed=moved, transcendentals=0),
    )(*operands)


def body(frames_in, norm_gain, w_qkv, w_out):
    x, z, c = lax.axis_index("x"), lax.axis_index("z"), lax.axis_index("c")
    place = jnp.stack([x, z, c]).astype(jnp.int32)
    gain = norm_gain.reshape(4, 1, QUARTER)

    slots = kernel_call(
        slice_kernel,
        [jax.ShapeDtypeStruct((96, 3 * HD), BF16)] * 4,
        (place, w_qkv.transpose(1, 0, 2)),
        0,
        6 * 10**5,
        4,
    )
    w_rows = [slots[0]] + [lax.ppermute(slots[k], "x", ring(4, k)) for k in (1, 2, 3)]
    w_rows = jnp.stack(w_rows)

    tokens = frames_in.reshape(16, 16, QUARTER)
    xa = lax.all_to_all(tokens, ("y", "c"), 0, 0, tiled=True).reshape(8, 32, QUARTER)
    xa, w_rows = lax.optimization_barrier((xa, w_rows))
    w_rows = lax.all_gather(w_rows, ("c", "y"), axis=1, tiled=True)
    xb = swap(xa, "z")
    la, ra = (lax.ppermute(xa, "x", ring(4, shift)) for shift in (1, 3))
    wo_give = lax.dynamic_slice_in_dim(after(w_out, xb), (1 - z) * 2 * QUARTER, 2 * QUARTER, axis=1)
    xb_late, wo_give = lax.optimization_barrier((xb, wo_give, la, ra))[:2]
    lb, rb = (lax.ppermute(xb_late, "x", ring(4, shift)) for shift in (1, 3))
    oa = lax.ppermute(jnp.where(c == 0, la, ra), ("x", "c"), across())
    ob = lax.ppermute(jnp.where(c == 0, lb, rb), ("x", "c"), across())

    def half(value, index, size):
        return lax.dynamic_slice_in_dim(value, index * size, size, axis=1)

    wo_keep = half(w_out, z, 2 * QUARTER)
    wo_got = swap(wo_give, "z")
    wo00, wo10 = half(wo_keep, c, QUARTER), half(wo_got, c, QUARTER)
    wo01, wo11 = swap(half(wo_keep, 1 - c, QUARTER), "c"), swap(half(wo_got, 1 - c, QUARTER), "c")

    attended = kernel_call(
        attend_kernel,
        jax.ShapeDtypeStruct((4, 8, 2, 16, 2 * HD), BF16),
        (place, xa, xb, la, lb, ra, rb, oa, ob, gain, w_rows),
        3 * 10**9,
        9 * 10**6,
        48,
        [
            pltpu.VMEM((512, WIDTH), BF16),
            pltpu.VMEM((WIDTH, 6 * HD), BF16),
            pltpu.VMEM((512, 6 * HD), F32),
            pltpu.SemaphoreType.DMA((8,)),
        ],
        left_out=(10,),
    )

    attended = lax.all_to_all(attended.reshape(64, 16, 2 * HD), ("x", "y", "z"), 0, 0, tiled=True)
    other = swap(attended, "c")
    shape = (4, 8, 2, 16, 2 * HD)
    mixed = kernel_call(
        output_kernel,
        jax.ShapeDtypeStruct((8, 2, 16, QUARTER), BF16),
        (
            place,
            attended.reshape(shape),
            other.reshape(shape),
            wo00,
            wo10,
            wo01,
            wo11,
            frames_in.reshape(8, 2, 16, QUARTER),
        ),
        8 * 10**8,
        6 * 10**6,
        16,
    )
    return mixed.reshape(1, 1, 256, QUARTER)


def solution(mesh):
    fine = Mesh(mesh.devices.reshape(4, 8, 2, 2, 4), ("x", "y", "z", "c", "dp"))
    seq, tensor = ("x", "y"), ("z", "c")
    in_specs = (P("dp", seq, None, tensor), P(), P(seq, None, tensor), P(tensor, None))
    out_specs = P("dp", seq, None, tensor)
    return jax.shard_map(body, mesh=fine, in_specs=in_specs, out_specs=out_specs, check_vma=False)
```
